32 devices in a mesh: rows: 4 (over y, x), half: 2 (over core), obs: 4 (over z).
Axes of the slice: x: 2, y: 2, z: 4, core: 2. Of those that a mesh axis runs over, the one named last changes fastest.
Arguments:
- ens_state: bfloat16 [2, 8192, 256], P('half', ('rows', 'obs')), may hold values from -6 to 6
- state_pos: bfloat16 [8192], P(('rows', 'obs')), may hold values from 0 to 1
- obs_ens: bfloat16 [2, 2, 8192, 256], P(None, 'half', ('rows', 'obs')), may hold values from -6 to 6
- obs_pos: bfloat16 [2, 8192], P(None, ('rows', 'obs')), may hold values from 0 to 1
- innov_weight: bfloat16 [2, 2, 8192, 256], P(None, 'half', ('rows', 'obs')), may hold values from -0.875 to 0.875
- block_rows: int32 [2, 64, 16], replicated, may hold values from 0 to 63, as said below
Outputs:
- increment: float32 [2, 8192, 256], P('half', ('rows', 'obs'))
The draws below stay inside these ranges and needn't reach their ends.
Inputs may be any that keep to these rules, and one draw needn't show every extreme that they name: `block_rows`: each row lists 16 different state blocks. Counting state blocks in aligned ranges of 16, an observation block names at most 8 blocks of one range, and in every aligned group of 16 observation blocks some range is named exactly 8 times by each block of the group.
All inputs are finite; a program needn't handle non-finite values.
Results may differ from the reference program's by a relative error of at most 0.0029.
Values may be sent and summed in bfloat16 or wider, within the bound.
A program may use at most 64 MiB of HBM per device.

```python
import jax
import jax.numpy as jnp
from jax import lax

BLOCK = 128
MEMBERS = 256
ROW_BLOCKS = 16
OBS_BLOCKS = 16
BATCHES = 2
ALL_ROW_BLOCKS = 64
ALL_OBS_BLOCKS = 64
STATE_ROWS = 8192
OBSERVATIONS = 8192
N_ROWS = 4
N_OBS = 4


def draw_block_rows(key, part):
    half_cap = ROW_BLOCKS // 2
    block_count = OBS_BLOCKS * N_OBS
    range_count = N_ROWS
    key_busy, key_cuts, key_order = jax.random.split(key, 3)
    busy_range = jax.random.randint(key_busy, (BATCHES, N_OBS), 0, range_count)
    busy_range = jnp.repeat(busy_range, OBS_BLOCKS, axis=1)
    cut_points = jnp.sort(jax.random.randint(key_cuts, (BATCHES, block_count, 2), 0, half_cap + 1), axis=-1)
    spread = jnp.stack([cut_points[..., 0], cut_points[..., 1] - cut_points[..., 0], half_cap - cut_points[..., 1]], axis=-1)
    range_iota = jnp.arange(range_count, dtype=jnp.int32)
    is_busy = range_iota[None, None, :] == busy_range[..., None]
    other_rank = range_iota[None, None, :] - (range_iota[None, None, :] > busy_range[..., None]).astype(jnp.int32)
    other_rank = jnp.clip(other_rank, 0, 2)
    counts = jnp.where(is_busy, half_cap, jnp.take_along_axis(spread, other_rank, axis=-1))
    scores = jax.random.randint(key_order, (BATCHES, block_count, range_count, ROW_BLOCKS), 0, 1 << 20) * ROW_BLOCKS + jnp.arange(ROW_BLOCKS, dtype=jnp.int32)
    shuffled = jnp.argsort(scores, axis=-1).astype(jnp.int32)[..., :half_cap]
    candidates = range_iota[None, None, :, None] * ROW_BLOCKS + shuffled
    alive_mask = jnp.arange(half_cap, dtype=jnp.int32)[None, None, None, :] < counts[..., None]
    candidates = candidates.reshape(BATCHES, block_count, range_count * half_cap)
    alive_mask = alive_mask.reshape(BATCHES, block_count, range_count * half_cap)
    ranking = jnp.where(alive_mask, 0, 1) * (range_count * half_cap) + jnp.arange(range_count * half_cap, dtype=jnp.int32)
    selection = jnp.argsort(ranking, axis=-1)[..., :ROW_BLOCKS * N_ROWS // 4]
    return jnp.take_along_axis(candidates, selection, axis=-1).astype(jnp.int32)


def shard_levels(key, dims, shards, low, high):
    def one(dim, shards_of):
        heights = jax.random.uniform(jax.random.fold_in(jax.random.fold_in(key, 6), dim), (shards_of,), jnp.float32, low / len(shards), high / len(shards))
        return jnp.repeat(jnp.exp(heights), dims[dim] // shards_of).reshape((-1,) + (1,) * (len(dims) - dim - 1))

    gain = one(*shards[0])
    for cut in shards[1:]:
        gain = gain * one(*cut)
    return gain


def normal_values(own_key, dims, scale, limit, cuts=(), held_as=jnp.bfloat16):
    gain = shard_levels(own_key, dims, cuts, -0.22, 0.18) if cuts else 1.0
    drawn = jax.random.normal(own_key, dims, jnp.float32) * scale * gain
    return jnp.minimum(jnp.maximum(drawn, -limit), limit).astype(held_as)


def setup_inputs(seed: int = 0) -> dict:
    seeds = jax.random.split(jax.random.key(seed), 7)
    ens_state = normal_values(seeds[0], (2, STATE_ROWS, MEMBERS), 1.0, 6.0, ((0, 2), (1, 16)))
    state_pos = jnp.clip(1.0 * jax.random.uniform(seeds[1], (STATE_ROWS,), jnp.float32) ** shard_levels(seeds[1], (STATE_ROWS,), ((0, 16),), -0.2, 0.2), 0.0, 1.0).astype(jnp.bfloat16)
    obs_ens = normal_values(seeds[2], (BATCHES, 2, OBSERVATIONS, MEMBERS), 1.0, 6.0, ((1, 2), (2, 16)))
    obs_pos = jnp.clip(1.0 * jax.random.uniform(seeds[3], (BATCHES, OBSERVATIONS), jnp.float32) ** shard_levels(seeds[3], (BATCHES, OBSERVATIONS), ((1, 16),), -0.2, 0.2), 0.0, 1.0).astype(jnp.bfloat16)
    innov_weight = normal_values(seeds[4], (BATCHES, 2, OBSERVATIONS, MEMBERS), 0.15, 0.875, ((1, 2), (2, 16)))
    block_rows = draw_block_rows(jax.random.fold_in(seeds[6], 71), 0)
    return {"ens_state": ens_state, "state_pos": state_pos, "obs_ens": obs_ens, "obs_pos": obs_pos, "innov_weight": innov_weight, "block_rows": block_rows}


def reference(ens_state, state_pos, obs_ens, obs_pos, innov_weight, block_rows):
    member_count = ens_state.shape[2]
    place_tiles = state_pos.astype(jnp.float32).reshape(ALL_ROW_BLOCKS, BLOCK)
    results = []
    for target in range(2):
        source = 1 - target
        state_tiles = ens_state[source].reshape(ALL_ROW_BLOCKS, BLOCK, member_count)

        def visit(running, entries, state_tiles=state_tiles):
            obs_tile, obs_place, weight_tile, named = entries
            gathered = state_tiles[named].reshape(-1, member_count)
            positions = place_tiles[named].reshape(-1)
            products = jnp.dot(gathered, obs_tile.T, preferred_element_type=jnp.float32)
            distance = positions[:, None] - obs_place[None, :]
            damping = jnp.exp(-4.0 * distance * distance)
            scaled = (products * damping / (member_count - 1)).astype(jnp.bfloat16)
            additions = jnp.dot(scaled, weight_tile, preferred_element_type=jnp.float32)
            running = running.at[named].add(additions.reshape(-1, BLOCK, member_count))
            return running, None

        running = jnp.zeros((ALL_ROW_BLOCKS, BLOCK, member_count), jnp.float32)
        for batch_index in range(BATCHES):
            entries = (obs_ens[batch_index, source].reshape(ALL_OBS_BLOCKS, BLOCK, member_count),
                       obs_pos[batch_index].astype(jnp.float32).reshape(ALL_OBS_BLOCKS, BLOCK),
                       innov_weight[batch_index, target].reshape(ALL_OBS_BLOCKS, BLOCK, member_count),
                       block_rows[batch_index].astype(jnp.int32))
            running, _ = lax.scan(visit, running, entries)
        results.append(running.reshape(STATE_ROWS, member_count))
    return jnp.stack(results)
```

```python
import functools
import math

import jax
import jax.numpy as jnp
from jax import lax
from jax.experimental import pallas as pl
from jax.experimental.pallas import tpu as pltpu
from jax.sharding import PartitionSpec as P

LANES = 128
UNIT = 256
STRETCH = 2.0 * math.sqrt(math.log2(math.e))
MASKED = -1e30


def kernel(sizes, state_ref, place_ref, obs_ref, obs_place_ref, weight_ref, named_ref, out_ref,
           states, columns, obs, weights, places, place_send, obs_places, obs_place_send, masks, total, shares, arrived,
           state_s, state_r, place_s, place_r, obs_s, obs_r, weight_s, weight_r, op_s, op_r, share_s, share_r, own_sem):
    n_rows, n_obs, own_rows, obs_rows, blocks, batches = sizes
    edge = obs_rows // blocks
    members = state_ref.shape[-1]
    span = n_obs * own_rows
    span_blocks = span // edge
    r, h, o = lax.axis_index("rows"), lax.axis_index("half"), lax.axis_index("obs")
    flip = 1 - h
    forward = n_rows == 4
    direct = (1, 2) if forward else tuple(range(1, n_rows))

    def at(row, half, column):
        return {"rows": row, "half": half, "obs": column}

    def remote(src, dst, send, recv, device):
        return pltpu.make_async_remote_copy(src_ref=src, dst_ref=dst, send_sem=send, recv_sem=recv,
                                            device_id=device, device_id_type=pl.DeviceIdType.MESH)

    def other(k):
        return lax.rem(o + k, n_obs)

    place_send[...] = place_ref[...].astype(jnp.float32) * STRETCH
    obs_place_send[...] = obs_place_ref[...].astype(jnp.float32) * STRETCH
    places[o] = place_send[...]
    obs_places[0] = obs_place_send[...]

    barrier = pltpu.get_barrier_semaphore()

    def greet(device):
        pl.semaphore_signal(barrier, inc=1, device_id=device, device_id_type=pl.DeviceIdType.MESH)

    greet(at(r, flip, o))
    for k in range(1, n_obs):
        greet(at(r, h, other(k)))
        greet(at(r, flip, other(k)))
    for delta in range(1, n_rows):
        greet(at(r ^ delta, h, o))
        greet(at(r ^ delta, flip, o))
    pl.semaphore_wait(barrier, 1 + 2 * (n_obs - 1) + 2 * (n_rows - 1))

    def state_slot(source):
        return states.at[pl.ds(pl.multiple_of(source * own_rows, own_rows), own_rows)]

    def state_copy(k):
        return remote(state_ref.at[0], state_slot(o), state_s.at[k], state_r.at[k], at(r, flip, other(k)))

    def state_arrival(k):
        source = lax.rem(o - k + n_obs, n_obs)
        return remote(state_ref.at[0], state_slot(source), state_s.at[k], state_r.at[k], at(r, flip, other(k)))

    def place_copy(k):
        return remote(place_send, places.at[o], place_s.at[k], place_r.at[k], at(r, h, other(k)))

    def place_arrival(k):
        source = lax.rem(o - k + n_obs, n_obs)
        return remote(place_send, places.at[source], place_s.at[k], place_r.at[k], at(r, h, other(k)))

    def obs_copy(delta, t):
        return remote(obs_ref.at[t, 0], obs.at[delta, t], obs_s.at[delta, t], obs_r.at[delta, t], at(r ^ delta, flip, o))

    def weight_copy(delta, t):
        return remote(weight_ref.at[t, 0], weights.at[delta, t], weight_s.at[delta, t], weight_r.at[delta, t],
                      at(r ^ delta, h, o))

    def obs_place_copy(delta):
        return remote(obs_place_send, obs_places.at[delta], op_s.at[delta], op_r.at[delta], at(r ^ delta, h, o))

    def obs_forward(t):
        came, goes = (1, 2) if t % 2 == 0 else (2, 1)
        return remote(obs.at[came, t], obs.at[3, t], obs_s.at[3, t], obs_r.at[3, t], at(r ^ goes, h, o))

    def weight_forward(t):
        came, goes = (1, 2) if t % 2 == 0 else (2, 1)
        return remote(weights.at[came, t], weights.at[3, t], weight_s.at[3, t], weight_r.at[3, t], at(r ^ goes, h, o))

    own_weights = [pltpu.make_async_copy(weight_ref.at[t, 0], weights.at[0, t], own_sem.at[t]) for t in range(batches)]

    for k in range(1, n_obs):
        place_copy(k).start()
    for delta in range(1, n_rows):
        obs_place_copy(delta).start()
    order = {1: [t for t in range(batches) if t % 2 == 0] + [t for t in range(batches) if t % 2],
             2: [t for t in range(batches) if t % 2] + [t for t in range(batches) if t % 2 == 0]}
    for step in range(batches):
        for delta in direct:
            t = order[delta][step] if delta in order else step
            obs_copy(delta, t).start()
            weight_copy(delta, t).start()
        if step == 0:
            state_copy(0).start()
            for t in range(batches):
                obs_copy(0, t).start()
                own_weights[t].start()
            for k in range(1, n_obs):
                state_copy(k).start()

    kept = -math.log2(members - 1)
    first = r * span_blocks
    ids = lax.broadcasted_iota(jnp.int32, (span_blocks, 1), 0) + first
    for delta in range(n_rows):
        base = ((r ^ delta) * n_obs + o) * blocks
        for t in range(batches):
            def fill(b, carry, base=base, delta=delta, t=t):
                named = named_ref[t, pl.ds(base + b, 1), :]
                listed = jnp.max(jnp.where(named == ids, 1.0, 0.0), axis=1, keepdims=True)
                masks[delta, t, b] = jnp.broadcast_to(jnp.where(listed > 0.5, kept, MASKED), (span_blocks, edge))
                return carry
            lax.fori_loop(0, blocks, fill, 0)

    total[...] = jnp.zeros_like(total)

    for k in range(1, n_obs):
        place_arrival(k).wait_recv()
    for delta in range(1, n_rows):
        obs_place_copy(delta).wait_recv()

    def stand(source, carry):
        for piece in range(-(-own_rows // LANES)):
            count = min(LANES, own_rows - piece * LANES)
            row = places[source, :, piece * LANES:(piece + 1) * LANES]
            column = jnp.broadcast_to(row, (LANES, LANES)).T
            start = pl.multiple_of(source * own_rows, own_rows) + piece * LANES
            columns[pl.ds(start, count), :] = column[:count]
        return carry
    lax.fori_loop(0, n_obs, stand, 0)

    def unit(delta, t, index):
        start = pl.multiple_of(index * UNIT, UNIT)
        products = lax.dot_general(states[pl.ds(start, UNIT), :], obs[delta, t], (((1,), (1,)), ((), ())),
                                   preferred_element_type=jnp.float32)
        parts = []
        for b in range(blocks):
            y = obs_places[delta, t, :, b * edge:(b + 1) * edge]
            rows = []
            for q in range(UNIT // edge):
                x = columns[pl.ds(start + q * edge, edge), :]
                m = masks[delta, t, b, pl.ds(index * (UNIT // edge) + q, 1), :]
                d = x - y
                damping = jnp.exp2(m - d * d)
                rows.append((products[q * edge:(q + 1) * edge, b * edge:(b + 1) * edge] * damping).astype(jnp.bfloat16))
            parts.append(jnp.concatenate(rows, axis=0))
        tiles = jnp.concatenate(parts, axis=1)
        total[pl.ds(start, UNIT), :] += jnp.dot(tiles, weights[delta, t], preferred_element_type=jnp.float32)

    def pieces_in(delta, t):
        obs_copy(delta, t).wait_recv()
        if delta:
            weight_copy(delta, t).wait_recv()
        else:
            own_weights[t].wait()

    if forward:
        for t in range(batches):
            came = 1 if t % 2 == 0 else 2
            pieces_in(came, t)
            obs_forward(t).start()
            weight_forward(t).start()
        done = {(1 if t % 2 == 0 else 2, t) for t in range(batches)}
    else:
        done = set()

    for k in range(n_obs):
        state_arrival(k).wait_recv()

    chunks = [(0, t) for t in range(batches)] + sorted(done)
    chunks += [(d, t) for d in range(1, n_rows) for t in range(batches) if (d, t) not in done]
    last = chunks[-batches:]
    for chunk in chunks[:-batches]:
        if chunk not in done:
            pieces_in(*chunk)

        def sweep(index, carry, chunk=chunk):
            unit(*chunk, index)
            return carry
        lax.fori_loop(0, span // UNIT, sweep, 0)

    for chunk in last:
        if chunk not in done:
            pieces_in(*chunk)

    group = max(UNIT, own_rows)
    groups = span // group
    own_group = o // (group // own_rows)

    def share_copy(d):
        return remote(shares.at[pl.ds(pl.multiple_of(d * own_rows, own_rows), own_rows)], arrived.at[o],
                      share_s.at[d], share_r.at[o], at(r, h, d))

    def finish(g, carry):
        which = lax.rem(own_group + 1 + g, groups)
        for u in range(group // UNIT):
            for chunk in last:
                unit(*chunk, which * (group // UNIT) + u)
        start = pl.multiple_of(which * group, group)
        shares[pl.ds(start, group), :] = total[pl.ds(start, group), :].astype(jnp.bfloat16)
        for j in range(group // own_rows):
            d = which * (group // own_rows) + j

            @pl.when(d != o)
            def _():
                share_copy(d).start()
        return carry
    lax.fori_loop(0, groups, finish, 0)

    mine = pl.multiple_of(o * own_rows, own_rows)

    out_ref[0] = total[pl.ds(mine, own_rows), :]

    def collect(k, carry):
        source = other(k)
        remote(shares.at[pl.ds(mine, own_rows)], arrived.at[source], share_s.at[source], share_r.at[source],
               at(r, h, source)).wait_recv()
        out_ref[0] += arrived[source].astype(jnp.float32)
        return carry
    lax.fori_loop(1, n_obs, collect, 0)

    def left(k, carry):
        share_copy(other(k)).wait_send()
        return carry
    lax.fori_loop(1, n_obs, left, 0)
    for k in range(n_obs):
        state_copy(k).wait_send()
        if k:
            place_copy(k).wait_send()
    for delta in range(n_rows):
        if delta:
            obs_place_copy(delta).wait_send()
        for t in range(batches):
            if delta == 0 or delta in direct:
                obs_copy(delta, t).wait_send()
                if delta:
                    weight_copy(delta, t).wait_send()
    if forward:
        for t in range(batches):
            obs_forward(t).wait_send()
            weight_forward(t).wait_send()


def local(mesh_shape, ens_state, state_pos, obs_ens, obs_pos, innov_weight, block_rows):
    n_rows, n_obs = mesh_shape["rows"], mesh_shape["obs"]
    own_rows, members = ens_state.shape[1:]
    batches, _, obs_rows, _ = obs_ens.shape
    blocks = block_rows.shape[1] // (n_rows * n_obs)
    edge = obs_rows // blocks
    span = n_obs * own_rows
    sizes = (n_rows, n_obs, own_rows, obs_rows, blocks, batches)
    place_row = state_pos[None, :]
    width = -(-own_rows // LANES) * LANES
    if width != own_rows:
        place_row = jnp.pad(place_row, ((0, 0), (0, width - own_rows)))
    dma = pltpu.SemaphoreType.DMA
    f32, bf16 = jnp.float32, jnp.bfloat16
    whole = pl.BlockSpec(memory_space=pltpu.VMEM)
    hbm = pl.BlockSpec(memory_space=pl.ANY)
    return pl.pallas_call(
        functools.partial(kernel, sizes),
        out_shape=jax.ShapeDtypeStruct(ens_state.shape, f32),
        in_specs=[hbm, whole, hbm, whole, hbm, whole],
        out_specs=whole,
        scratch_shapes=[
            pltpu.VMEM((span, members), bf16),
            pltpu.VMEM((span, LANES), f32),
            pltpu.VMEM((n_rows, batches, obs_rows, members), bf16),
            pltpu.VMEM((n_rows, batches, obs_rows, members), bf16),
            pltpu.VMEM((n_obs, 1, width), f32),
            pltpu.VMEM((1, width), f32),
            pltpu.VMEM((n_rows, batches, 1, obs_rows), f32),
            pltpu.VMEM((batches, 1, obs_rows), f32),
            pltpu.VMEM((n_rows, batches, blocks, span // edge, edge), f32),
            pltpu.VMEM((span, members), f32),
            pltpu.VMEM((span, members), bf16),
            pltpu.VMEM((n_obs, own_rows, members), bf16),
            dma((n_obs,)), dma((n_obs,)), dma((n_obs,)), dma((n_obs,)),
            dma((n_rows, batches)), dma((n_rows, batches)), dma((n_rows, batches)), dma((n_rows, batches)),
            dma((n_rows,)), dma((n_rows,)), dma((n_obs,)), dma((n_obs,)), dma((batches,)),
        ],
        compiler_params=pltpu.CompilerParams(collective_id=0, has_side_effects=True, vmem_limit_bytes=48 * 2**20),
        cost_estimate=pl.CostEstimate(flops=4 * span * members * n_rows * batches * obs_rows,
                                      bytes_accessed=4 * 2**20,
                                      transcendentals=span * n_rows * batches * obs_rows),
    )(ens_state, place_row, obs_ens, obs_pos[:, None, :], innov_weight, block_rows)


def solution(mesh):
    in_specs = (
        P("half", ("rows", "obs"), None),
        P(("rows", "obs")),
        P(None, "half", ("rows", "obs"), None),
        P(None, ("rows", "obs")),
        P(None, "half", ("rows", "obs"), None),
        P(),
    )
    out_specs = P("half", ("rows", "obs"), None)
    return jax.shard_map(functools.partial(local, dict(mesh.shape)), mesh=mesh, in_specs=in_specs,
                         out_specs=out_specs, check_vma=False)
```

```python
import functools
import math

import jax
import jax.numpy as jnp
from jax import lax
from jax.experimental import pallas as pl
from jax.experimental.pallas import tpu as pltpu
from jax.sharding import PartitionSpec as P

LANES = 128
UNIT = 256
UNROLL = 4
STRETCH = 2.0 * math.sqrt(math.log2(math.e))
MASKED = -1e30


def kernel(sizes, state_ref, place_ref, obs_ref, obs_place_ref, weight_ref, named_ref, out_ref,
           states, columns, obs, weights, places, place_send, obs_places, obs_place_send, masks, total, shares, arrived,
           state_s, state_r, place_s, place_r, obs_s, obs_r, weight_s, weight_r, op_s, op_r, share_s, share_r, own_sem,
           hop, hop_sem):
    n_rows, n_obs, own_rows, obs_rows, blocks, batches = sizes
    edge = obs_rows // blocks
    members = state_ref.shape[-1]
    span = n_obs * own_rows
    span_blocks = span // edge
    r, h, o = lax.axis_index("rows"), lax.axis_index("half"), lax.axis_index("obs")
    flip = 1 - h
    forward = n_rows == 4
    direct = (1, 2) if forward else tuple(range(1, n_rows))

    def at(row, half, column):
        return {"rows": row, "half": half, "obs": column}

    def remote(src, dst, send, recv, device):
        return pltpu.make_async_remote_copy(src_ref=src, dst_ref=dst, send_sem=send, recv_sem=recv,
                                            device_id=device, device_id_type=pl.DeviceIdType.MESH)

    def other(k):
        return lax.rem(o + k, n_obs)

    place_send[...] = place_ref[...].astype(jnp.float32) * STRETCH
    obs_place_send[...] = obs_place_ref[...].astype(jnp.float32) * STRETCH
    places[o] = place_send[...]
    obs_places[0] = obs_place_send[...]

    barrier = pltpu.get_barrier_semaphore()

    def greet(device):
        pl.semaphore_signal(barrier, inc=1, device_id=device, device_id_type=pl.DeviceIdType.MESH)

    greet(at(r, flip, o))
    for k in range(1, n_obs):
        greet(at(r, h, other(k)))
        greet(at(r, flip, other(k)))
    for delta in range(1, n_rows):
        greet(at(r ^ delta, h, o))
        greet(at(r ^ delta, flip, o))
    pl.semaphore_wait(barrier, 1 + 2 * (n_obs - 1) + 2 * (n_rows - 1))

    def state_slot(source):
        return states.at[pl.ds(pl.multiple_of(source * own_rows, own_rows), own_rows)]

    def state_copy(k):
        return remote(state_ref.at[0], state_slot(o), state_s.at[k], state_r.at[k], at(r, flip, other(k)))

    def state_arrival(k):
        source = lax.rem(o - k + n_obs, n_obs)
        return remote(state_ref.at[0], state_slot(source), state_s.at[k], state_r.at[k], at(r, flip, other(k)))

    def place_copy(k):
        return remote(place_send, places.at[o], place_s.at[k], place_r.at[k], at(r, h, other(k)))

    def place_arrival(k):
        source = lax.rem(o - k + n_obs, n_obs)
        return remote(place_send, places.at[source], place_s.at[k], place_r.at[k], at(r, h, other(k)))

    def obs_copy(delta, t):
        return remote(obs_ref.at[t, 0], obs.at[delta, t], obs_s.at[delta, t], obs_r.at[delta, t], at(r ^ delta, flip, o))

    def weight_copy(delta, t):
        return remote(weight_ref.at[t, 0], weights.at[delta, t], weight_s.at[delta, t], weight_r.at[delta, t],
                      at(r ^ delta, h, o))

    def obs_place_copy(delta):
        return remote(obs_place_send, obs_places.at[delta], op_s.at[delta], op_r.at[delta], at(r ^ delta, h, o))

    def obs_forward(t):
        came, goes = (1, 2) if t % 2 == 0 else (2, 1)
        return remote(obs.at[came, t], obs.at[3, t], obs_s.at[3, t], obs_r.at[3, t], at(r ^ goes, h, o))

    def weight_forward(t):
        came, goes = (1, 2) if t % 2 == 0 else (2, 1)
        return remote(weights.at[came, t], weights.at[3, t], weight_s.at[3, t], weight_r.at[3, t], at(r ^ goes, h, o))

    own_weights = [pltpu.make_async_copy(weight_ref.at[t, 0], weights.at[0, t], own_sem.at[t]) for t in range(batches)]

    for k in range(1, n_obs):
        place_copy(k).start()
    for delta in range(1, n_rows):
        obs_place_copy(delta).start()
    order = {1: [t for t in range(batches) if t % 2 == 0] + [t for t in range(batches) if t % 2],
             2: [t for t in range(batches) if t % 2] + [t for t in range(batches) if t % 2 == 0]}
    for step in range(batches):
        for delta in direct:
            t = order[delta][step] if delta in order else step
            obs_copy(delta, t).start()
            weight_copy(delta, t).start()
        if step == 0:
            state_copy(0).start()
            for t in range(batches):
                obs_copy(0, t).start()
                own_weights[t].start()
            for k in range(1, n_obs):
                state_copy(k).start()

    kept = -math.log2(members - 1)
    first = r * span_blocks
    ids = lax.broadcasted_iota(jnp.int32, (span_blocks, 1), 0) + first
    for delta in range(n_rows):
        base = ((r ^ delta) * n_obs + o) * blocks
        for t in range(batches):
            def fill(b, carry, base=base, delta=delta, t=t):
                named = named_ref[t, pl.ds(base + b, 1), :]
                listed = jnp.max(jnp.where(named == ids, 1.0, 0.0), axis=1, keepdims=True)
                masks[delta, t, b] = jnp.broadcast_to(jnp.where(listed > 0.5, kept, MASKED), (span_blocks, edge))
                return carry
            lax.fori_loop(0, blocks, fill, 0)

    total[...] = jnp.zeros_like(total)

    for k in range(1, n_obs):
        place_arrival(k).wait_recv()
    for delta in range(1, n_rows):
        obs_place_copy(delta).wait_recv()

    def stand(source, carry):
        for piece in range(-(-own_rows // LANES)):
            count = min(LANES, own_rows - piece * LANES)
            row = places[source, :, piece * LANES:(piece + 1) * LANES]
            column = jnp.broadcast_to(row, (LANES, LANES)).T
            start = pl.multiple_of(source * own_rows, own_rows) + piece * LANES
            columns[pl.ds(start, count), :] = column[:count]
        return carry
    lax.fori_loop(0, n_obs, stand, 0)

    def unit(delta, t, index):
        start = pl.multiple_of(index * UNIT, UNIT)
        products = lax.dot_general(states[pl.ds(start, UNIT), :], obs[delta, t], (((1,), (1,)), ((), ())),
                                   preferred_element_type=jnp.float32)
        parts = []
        for b in range(blocks):
            y = obs_places[delta, t, :, b * edge:(b + 1) * edge]
            rows = []
            for q in range(UNIT // edge):
                x = columns[pl.ds(start + q * edge, edge), :]
                m = masks[delta, t, b, pl.ds(index * (UNIT // edge) + q, 1), :]
                d = x - y
                damping = jnp.exp2(m - d * d)
                rows.append((products[q * edge:(q + 1) * edge, b * edge:(b + 1) * edge] * damping).astype(jnp.bfloat16))
            parts.append(jnp.concatenate(rows, axis=0))
        tiles = jnp.concatenate(parts, axis=1)
        total[pl.ds(start, UNIT), :] += jnp.dot(tiles, weights[delta, t], preferred_element_type=jnp.float32)

    def pieces_in(delta, t):
        obs_copy(delta, t).wait_recv()
        if delta:
            weight_copy(delta, t).wait_recv()
        else:
            own_weights[t].wait()

    per_source = own_rows // UNIT
    early = [(0, t) for t in range(batches)] if per_source else []

    def sweep(chunk, first_unit, count):
        def step(i, carry):
            unit(*chunk, first_unit + i)
            return carry
        lax.fori_loop(0, count, step, 0, unroll=math.gcd(count, UNROLL))

    def early_source(k):
        state_arrival(k).wait_recv()
        for u in range(per_source):
            for chunk in early:
                unit(*chunk, lax.rem(o - k + n_obs, n_obs) * per_source + u)

    for chunk in early:
        pieces_in(*chunk)
    early_source(0)

    if forward:
        for t in range(batches):
            came = 1 if t % 2 == 0 else 2
            pieces_in(came, t)
            obs_forward(t).start()
            weight_forward(t).start()
        done = {(1 if t % 2 == 0 else 2, t) for t in range(batches)}
    else:
        done = set()

    for k in sorted(range(1, n_obs), key=lambda k: min(k, n_obs - k)):
        early_source(k)
    done.update(early)

    chunks = sorted(done - set(early))
    chunks += [(d, t) for d in range(n_rows) for t in range(batches) if (d, t) not in done]
    last = chunks[-batches:]
    for chunk in chunks[:-batches]:
        if chunk not in done:
            pieces_in(*chunk)
        sweep(chunk, 0, span // UNIT)

    for chunk in last:
        if chunk not in done:
            pieces_in(*chunk)

    group = max(UNIT, own_rows)
    groups = span // group
    own_group = o // (group // own_rows)

    def share_copy(d):
        return remote(shares.at[pl.ds(pl.multiple_of(d * own_rows, own_rows), own_rows)], arrived.at[o],
                      share_s.at[d], share_r.at[o], at(r, h, d))

    relay = n_obs == 4 and group == own_rows
    mirror = o // 2
    inner = o + mirror * (3 - 2 * o)

    def hop_copy(d):
        return remote(shares.at[pl.ds(pl.multiple_of(d * own_rows, own_rows), own_rows)], hop, hop_sem.at[0],
                      hop_sem.at[1], at(r, h, 1 + mirror))

    def finish(g, carry):
        if relay:
            towards = (1 - inner) * (3 - g) + inner * lax.rem(2 + 3 * g, 5)
            which = towards + mirror * (3 - 2 * towards)
        else:
            which = lax.rem(own_group + 1 + g, groups)
        for u in range(group // UNIT):
            for chunk in last:
                unit(*chunk, which * (group // UNIT) + u)
        start = pl.multiple_of(which * group, group)
        if relay:
            apart = (which - o) * (which - o)

            @pl.when(apart == 9)
            def _():
                shares[pl.ds(start, group), :] = total[pl.ds(start, group), :].astype(jnp.bfloat16)
                hop_copy(which).start()

            @pl.when((apart == 4) & (inner == 1))
            def _():
                hop_copy(which).wait_recv()
                shares[pl.ds(start, group), :] = (
                    total[pl.ds(start, group), :] + hop[...].astype(jnp.float32)).astype(jnp.bfloat16)
                share_copy(which).start()

            @pl.when((apart == 1) | ((apart == 4) & (inner == 0)))
            def _():
                shares[pl.ds(start, group), :] = total[pl.ds(start, group), :].astype(jnp.bfloat16)
                share_copy(which).start()
            return carry
        shares[pl.ds(start, group), :] = total[pl.ds(start, group), :].astype(jnp.bfloat16)
        for j in range(group // own_rows):
            d = which * (group // own_rows) + j

            @pl.when(d != o)
            def _():
                share_copy(d).start()
        return carry
    lax.fori_loop(0, groups, finish, 0)

    mine = pl.multiple_of(o * own_rows, own_rows)

    out_ref[0] = total[pl.ds(mine, own_rows), :]

    def collect(k, carry):
        source = other(k)

        def take():
            remote(shares.at[pl.ds(mine, own_rows)], arrived.at[source], share_s.at[source], share_r.at[source],
                   at(r, h, source)).wait_recv()
            out_ref[0] += arrived[source].astype(jnp.float32)
        if relay:
            pl.when((source - o) * (source - o) != 9)(take)
        else:
            take()
        return carry
    lax.fori_loop(1, n_obs, collect, 0)

    def left(k, carry):
        d = other(k)
        if relay:
            @pl.when((d - o) * (d - o) == 9)
            def _():
                hop_copy(d).wait_send()

            @pl.when((d - o) * (d - o) != 9)
            def _():
                share_copy(d).wait_send()
        else:
            share_copy(d).wait_send()
        return carry
    lax.fori_loop(1, n_obs, left, 0)
    for k in range(n_obs):
        state_copy(k).wait_send()
        if k:
            place_copy(k).wait_send()
    for delta in range(n_rows):
        if delta:
            obs_place_copy(delta).wait_send()
        for t in range(batches):
            if delta == 0 or delta in direct:
                obs_copy(delta, t).wait_send()
                if delta:
                    weight_copy(delta, t).wait_send()
    if forward:
        for t in range(batches):
            obs_forward(t).wait_send()
            weight_forward(t).wait_send()


def local(mesh_shape, ens_state, state_pos, obs_ens, obs_pos, innov_weight, block_rows):
    n_rows, n_obs = mesh_shape["rows"], mesh_shape["obs"]
    own_rows, members = ens_state.shape[1:]
    batches, _, obs_rows, _ = obs_ens.shape
    blocks = block_rows.shape[1] // (n_rows * n_obs)
    edge = obs_rows // blocks
    span = n_obs * own_rows
    sizes = (n_rows, n_obs, own_rows, obs_rows, blocks, batches)
    place_row = state_pos[None, :]
    width = -(-own_rows // LANES) * LANES
    if width != own_rows:
        place_row = jnp.pad(place_row, ((0, 0), (0, width - own_rows)))
    dma = pltpu.SemaphoreType.DMA
    f32, bf16 = jnp.float32, jnp.bfloat16
    whole = pl.BlockSpec(memory_space=pltpu.VMEM)
    hbm = pl.BlockSpec(memory_space=pltpu.HBM)
    return pl.pallas_call(
        functools.partial(kernel, sizes),
        out_shape=jax.ShapeDtypeStruct(ens_state.shape, f32),
        in_specs=[hbm, whole, hbm, whole, hbm, whole],
        out_specs=whole,
        scratch_shapes=[
            pltpu.VMEM((span, members), bf16),
            pltpu.VMEM((span, LANES), f32),
            pltpu.VMEM((n_rows, batches, obs_rows, members), bf16),
            pltpu.VMEM((n_rows, batches, obs_rows, members), bf16),
            pltpu.VMEM((n_obs, 1, width), f32),
            pltpu.VMEM((1, width), f32),
            pltpu.VMEM((n_rows, batches, 1, obs_rows), f32),
            pltpu.VMEM((batches, 1, obs_rows), f32),
            pltpu.VMEM((n_rows, batches, blocks, span // edge, edge), f32),
            pltpu.VMEM((span, members), f32),
            pltpu.VMEM((span, members), bf16),
            pltpu.VMEM((n_obs, own_rows, members), bf16),
            dma((n_obs,)), dma((n_obs,)), dma((n_obs,)), dma((n_obs,)),
            dma((n_rows, batches)), dma((n_rows, batches)), dma((n_rows, batches)), dma((n_rows, batches)),
            dma((n_rows,)), dma((n_rows,)), dma((n_obs,)), dma((n_obs,)), dma((batches,)),
            pltpu.VMEM((own_rows, members), bf16), dma((2,)),
        ],
        compiler_params=pltpu.CompilerParams(collective_id=0, has_side_effects=True, vmem_limit_bytes=40 * 2**20),
        cost_estimate=pl.CostEstimate(flops=4 * span * members * n_rows * batches * obs_rows,
                                      bytes_accessed=4 * 2**20,
                                      transcendentals=span * n_rows * batches * obs_rows),
    )(ens_state, place_row, obs_ens, obs_pos[:, None, :], innov_weight, block_rows)


def solution(mesh):
    in_specs = (
        P("half", ("rows", "obs"), None),
        P(("rows", "obs")),
        P(None, "half", ("rows", "obs"), None),
        P(None, ("rows", "obs")),
        P(None, "half", ("rows", "obs"), None),
        P(),
    )
    out_specs = P("half", ("rows", "obs"), None)
    return jax.shard_map(functools.partial(local, dict(mesh.shape)), mesh=mesh, in_specs=in_specs,
                         out_specs=out_specs, check_vma=False)
```

```python
import functools
import math

import jax
import jax.numpy as jnp
from jax import lax
from jax.experimental import pallas as pl
from jax.experimental.pallas import tpu as pltpu
from jax.sharding import PartitionSpec as P

LANES = 128
UNIT = 256
UNROLL = 4
STRETCH = 2.0 * math.sqrt(math.log2(math.e))
MASKED = -1e30


def kernel(sizes, state_ref, place_ref, obs_ref, obs_place_ref, weight_ref, named_ref, out_ref,
           states, columns, obs, weights, places, place_send, obs_places, obs_place_send, masks, total, shares, arrived,
           state_s, state_r, place_s, place_r, obs_s, obs_r, weight_s, weight_r, op_s, op_r, share_s, share_r, own_sem,
           hop, hop_sem):
    n_rows, n_obs, own_rows, obs_rows, blocks, batches = sizes
    edge = obs_rows // blocks
    members = state_ref.shape[-1]
    span = n_obs * own_rows
    span_blocks = span // edge
    r, h, o = lax.axis_index("rows"), lax.axis_index("half"), lax.axis_index("obs")
    flip = 1 - h
    forward = n_rows == 4
    direct = (1, 2) if forward else tuple(range(1, n_rows))

    def at(row, half, column):
        return {"rows": row, "half": half, "obs": column}

    def remote(src, dst, send, recv, device):
        return pltpu.make_async_remote_copy(src_ref=src, dst_ref=dst, send_sem=send, recv_sem=recv,
                                            device_id=device, device_id_type=pl.DeviceIdType.MESH)

    def other(k):
        return lax.rem(o + k, n_obs)

    place_send[...] = place_ref[...].astype(jnp.float32) * STRETCH
    obs_place_send[...] = obs_place_ref[...].astype(jnp.float32) * STRETCH
    places[o] = place_send[...]
    obs_places[0] = obs_place_send[...]

    barrier = pltpu.get_barrier_semaphore()

    def greet(device):
        pl.semaphore_signal(barrier, inc=1, device_id=device, device_id_type=pl.DeviceIdType.MESH)

    greet(at(r, flip, o))
    for k in range(1, n_obs):
        greet(at(r, h, other(k)))
        greet(at(r, flip, other(k)))
    for delta in range(1, n_rows):
        greet(at(r ^ delta, h, o))
        greet(at(r ^ delta, flip, o))
    pl.semaphore_wait(barrier, 1 + 2 * (n_obs - 1) + 2 * (n_rows - 1))

    def state_slot(source):
        return states.at[pl.ds(pl.multiple_of(source * own_rows, own_rows), own_rows)]

    def state_copy(k):
        return remote(state_ref.at[0], state_slot(o), state_s.at[k], state_r.at[k], at(r, flip, other(k)))

    def state_arrival(k):
        source = lax.rem(o - k + n_obs, n_obs)
        return remote(state_ref.at[0], state_slot(source), state_s.at[k], state_r.at[k], at(r, flip, other(k)))

    def place_copy(k):
        return remote(place_send, places.at[o], place_s.at[k], place_r.at[k], at(r, h, other(k)))

    def place_arrival(k):
        source = lax.rem(o - k + n_obs, n_obs)
        return remote(place_send, places.at[source], place_s.at[k], place_r.at[k], at(r, h, other(k)))

    def obs_copy(delta, t):
        return remote(obs_ref.at[t, 0], obs.at[delta, t], obs_s.at[delta, t], obs_r.at[delta, t], at(r ^ delta, flip, o))

    def weight_copy(delta, t):
        return remote(weight_ref.at[t, 0], weights.at[delta, t], weight_s.at[delta, t], weight_r.at[delta, t],
                      at(r ^ delta, h, o))

    def obs_place_copy(delta):
        return remote(obs_place_send, obs_places.at[delta], op_s.at[delta], op_r.at[delta], at(r ^ delta, h, o))

    def obs_forward(t):
        came, goes = (1, 2) if t % 2 == 0 else (2, 1)
        return remote(obs.at[came, t], obs.at[3, t], obs_s.at[3, t], obs_r.at[3, t], at(r ^ goes, h, o))

    def weight_forward(t):
        came, goes = (1, 2) if t % 2 == 0 else (2, 1)
        return remote(weights.at[came, t], weights.at[3, t], weight_s.at[3, t], weight_r.at[3, t], at(r ^ goes, h, o))

    own_weights = [pltpu.make_async_copy(weight_ref.at[t, 0], weights.at[0, t], own_sem.at[t]) for t in range(batches)]

    for k in range(1, n_obs):
        place_copy(k).start()
    for delta in range(1, n_rows):
        obs_place_copy(delta).start()
    order = {1: [t for t in range(batches) if t % 2 == 0] + [t for t in range(batches) if t % 2],
             2: [t for t in range(batches) if t % 2] + [t for t in range(batches) if t % 2 == 0]}
    for step in range(batches):
        for delta in direct:
            t = order[delta][step] if delta in order else step
            obs_copy(delta, t).start()
            weight_copy(delta, t).start()
        if step == 0:
            state_copy(0).start()
            for t in range(batches):
                obs_copy(0, t).start()
                own_weights[t].start()
            for k in range(1, n_obs):
                state_copy(k).start()

    kept = -math.log2(members - 1)
    first = r * span_blocks
    lanes = lax.broadcasted_iota(jnp.int32, (1, named_ref.shape[-1]), 1)
    lists = [jnp.concatenate([jnp.max(jnp.where(named_ref[t] == first + i, 1.0, 0.0), axis=0, keepdims=True)
                              for i in range(span_blocks)], axis=0) for t in range(batches)]
    for delta in range(n_rows):
        base = ((r ^ delta) * n_obs + o) * blocks
        for t in range(batches):
            def fill(b, carry, base=base, delta=delta, t=t):
                listed = jnp.max(jnp.where(lanes == base + b, lists[t], 0.0), axis=1, keepdims=True)
                masks[delta, t, b] = jnp.broadcast_to(jnp.where(listed > 0.5, kept, MASKED), (span_blocks, edge))
                return carry
            lax.fori_loop(0, blocks, fill, 0)

    total[...] = jnp.zeros_like(total)

    for k in range(1, n_obs):
        place_arrival(k).wait_recv()
    for delta in range(1, n_rows):
        obs_place_copy(delta).wait_recv()

    def stand(source, carry):
        for piece in range(-(-own_rows // LANES)):
            count = min(LANES, own_rows - piece * LANES)
            row = places[source, :, piece * LANES:(piece + 1) * LANES]
            column = jnp.broadcast_to(row, (LANES, LANES)).T
            start = pl.multiple_of(source * own_rows, own_rows) + piece * LANES
            columns[pl.ds(start, count), :] = column[:count]
        return carry
    lax.fori_loop(0, n_obs, stand, 0)

    def unit(delta, t, index):
        start = pl.multiple_of(index * UNIT, UNIT)
        products = lax.dot_general(states[pl.ds(start, UNIT), :], obs[delta, t], (((1,), (1,)), ((), ())),
                                   preferred_element_type=jnp.float32)
        parts = []
        for b in range(blocks):
            y = obs_places[delta, t, :, b * edge:(b + 1) * edge]
            rows = []
            for q in range(UNIT // edge):
                x = columns[pl.ds(start + q * edge, edge), :]
                m = masks[delta, t, b, pl.ds(index * (UNIT // edge) + q, 1), :]
                d = x - y
                damping = jnp.exp2(m - d * d)
                rows.append((products[q * edge:(q + 1) * edge, b * edge:(b + 1) * edge] * damping).astype(jnp.bfloat16))
            parts.append(jnp.concatenate(rows, axis=0))
        tiles = jnp.concatenate(parts, axis=1)
        total[pl.ds(start, UNIT), :] += jnp.dot(tiles, weights[delta, t], preferred_element_type=jnp.float32)

    def pieces_in(delta, t):
        obs_copy(delta, t).wait_recv()
        if delta:
            weight_copy(delta, t).wait_recv()
        else:
            own_weights[t].wait()

    per_source = own_rows // UNIT
    early = [(0, t) for t in range(batches)] if per_source else []

    def sweep(chunk, first_unit, count):
        def step(i, carry):
            unit(*chunk, first_unit + i)
            return carry
        lax.fori_loop(0, count, step, 0, unroll=math.gcd(count, UNROLL))

    def early_source(k):
        state_arrival(k).wait_recv()
        for u in range(per_source):
            for chunk in early:
                unit(*chunk, lax.rem(o - k + n_obs, n_obs) * per_source + u)

    for chunk in early:
        pieces_in(*chunk)
    early_source(0)

    if forward:
        for t in range(batches):
            came = 1 if t % 2 == 0 else 2
            pieces_in(came, t)
            obs_forward(t).start()
            weight_forward(t).start()
        done = {(1 if t % 2 == 0 else 2, t) for t in range(batches)}
    else:
        done = set()

    for k in sorted(range(1, n_obs), key=lambda k: min(k, n_obs - k)):
        early_source(k)
    done.update(early)

    chunks = sorted(done - set(early))
    chunks += [(d, t) for d in range(n_rows) for t in range(batches) if (d, t) not in done]
    last = chunks[-batches:]
    for chunk in chunks[:-batches]:
        if chunk not in done:
            pieces_in(*chunk)
        sweep(chunk, 0, span // UNIT)

    for chunk in last:
        if chunk not in done:
            pieces_in(*chunk)

    group = max(UNIT, own_rows)
    groups = span // group
    own_group = o // (group // own_rows)

    def share_copy(d):
        return remote(shares.at[pl.ds(pl.multiple_of(d * own_rows, own_rows), own_rows)], arrived.at[o],
                      share_s.at[d], share_r.at[o], at(r, h, d))

    relay = n_obs == 4 and group == own_rows
    mirror = o // 2
    inner = o + mirror * (3 - 2 * o)

    def hop_copy(d):
        return remote(shares.at[pl.ds(pl.multiple_of(d * own_rows, own_rows), own_rows)], hop, hop_sem.at[0],
                      hop_sem.at[1], at(r, h, 1 + mirror))

    def finish(g, carry):
        if relay:
            towards = (1 - inner) * (3 - g) + inner * lax.rem(2 + 3 * g, 5)
            which = towards + mirror * (3 - 2 * towards)
        else:
            which = lax.rem(own_group + 1 + g, groups)
        for u in range(group // UNIT):
            for chunk in last:
                unit(*chunk, which * (group // UNIT) + u)
        start = pl.multiple_of(which * group, group)
        if relay:
            apart = (which - o) * (which - o)

            @pl.when(apart == 9)
            def _():
                shares[pl.ds(start, group), :] = total[pl.ds(start, group), :].astype(jnp.bfloat16)
                hop_copy(which).start()

            @pl.when((apart == 4) & (inner == 1))
            def _():
                hop_copy(which).wait_recv()
                shares[pl.ds(start, group), :] = (
                    total[pl.ds(start, group), :] + hop[...].astype(jnp.float32)).astype(jnp.bfloat16)
                share_copy(which).start()

            @pl.when((apart == 1) | ((apart == 4) & (inner == 0)))
            def _():
                shares[pl.ds(start, group), :] = total[pl.ds(start, group), :].astype(jnp.bfloat16)
                share_copy(which).start()
            return carry
        shares[pl.ds(start, group), :] = total[pl.ds(start, group), :].astype(jnp.bfloat16)
        for j in range(group // own_rows):
            d = which * (group // own_rows) + j

            @pl.when(d != o)
            def _():
                share_copy(d).start()
        return carry
    lax.fori_loop(0, groups, finish, 0)

    mine = pl.multiple_of(o * own_rows, own_rows)

    out_ref[0] = total[pl.ds(mine, own_rows), :]

    def collect(k, carry):
        source = other(k)

        def take():
            remote(shares.at[pl.ds(mine, own_rows)], arrived.at[source], share_s.at[source], share_r.at[source],
                   at(r, h, source)).wait_recv()
            out_ref[0] += arrived[source].astype(jnp.float32)
        if relay:
            pl.when((source - o) * (source - o) != 9)(take)
        else:
            take()
        return carry
    lax.fori_loop(1, n_obs, collect, 0)

    def left(k, carry):
        d = other(k)
        if relay:
            @pl.when((d - o) * (d - o) == 9)
            def _():
                hop_copy(d).wait_send()

            @pl.when((d - o) * (d - o) != 9)
            def _():
                share_copy(d).wait_send()
        else:
            share_copy(d).wait_send()
        return carry
    lax.fori_loop(1, n_obs, left, 0)
    for k in range(n_obs):
        state_copy(k).wait_send()
        if k:
            place_copy(k).wait_send()
    for delta in range(n_rows):
        if delta:
            obs_place_copy(delta).wait_send()
        for t in range(batches):
            if delta == 0 or delta in direct:
                obs_copy(delta, t).wait_send()
                if delta:
                    weight_copy(delta, t).wait_send()
    if forward:
        for t in range(batches):
            obs_forward(t).wait_send()
            weight_forward(t).wait_send()


def local(mesh_shape, ens_state, state_pos, obs_ens, obs_pos, innov_weight, block_rows):
    n_rows, n_obs = mesh_shape["rows"], mesh_shape["obs"]
    own_rows, members = ens_state.shape[1:]
    batches, _, obs_rows, _ = obs_ens.shape
    blocks = block_rows.shape[1] // (n_rows * n_obs)
    edge = obs_rows // blocks
    span = n_obs * own_rows
    sizes = (n_rows, n_obs, own_rows, obs_rows, blocks, batches)
    place_row = state_pos[None, :]
    width = -(-own_rows // LANES) * LANES
    if width != own_rows:
        place_row = jnp.pad(place_row, ((0, 0), (0, width - own_rows)))
    dma = pltpu.SemaphoreType.DMA
    f32, bf16 = jnp.float32, jnp.bfloat16
    whole = pl.BlockSpec(memory_space=pltpu.VMEM)
    hbm = pl.BlockSpec(memory_space=pltpu.HBM)
    return pl.pallas_call(
        functools.partial(kernel, sizes),
        out_shape=jax.ShapeDtypeStruct(ens_state.shape, f32),
        in_specs=[hbm, whole, hbm, whole, hbm, whole],
        out_specs=whole,
        scratch_shapes=[
            pltpu.VMEM((span, members), bf16),
            pltpu.VMEM((span, LANES), f32),
            pltpu.VMEM((n_rows, batches, obs_rows, members), bf16),
            pltpu.VMEM((n_rows, batches, obs_rows, members), bf16),
            pltpu.VMEM((n_obs, 1, width), f32),
            pltpu.VMEM((1, width), f32),
            pltpu.VMEM((n_rows, batches, 1, obs_rows), f32),
            pltpu.VMEM((batches, 1, obs_rows), f32),
            pltpu.VMEM((n_rows, batches, blocks, span // edge, edge), f32),
            pltpu.VMEM((span, members), f32),
            pltpu.VMEM((span, members), bf16),
            pltpu.VMEM((n_obs, own_rows, members), bf16),
            dma((n_obs,)), dma((n_obs,)), dma((n_obs,)), dma((n_obs,)),
            dma((n_rows, batches)), dma((n_rows, batches)), dma((n_rows, batches)), dma((n_rows, batches)),
            dma((n_rows,)), dma((n_rows,)), dma((n_obs,)), dma((n_obs,)), dma((batches,)),
            pltpu.VMEM((own_rows, members), bf16), dma((2,)),
        ],
        compiler_params=pltpu.CompilerParams(collective_id=0, has_side_effects=True, vmem_limit_bytes=40 * 2**20),
        cost_estimate=pl.CostEstimate(flops=4 * span * members * n_rows * batches * obs_rows,
                                      bytes_accessed=4 * 2**20,
                                      transcendentals=span * n_rows * batches * obs_rows),
    )(ens_state, place_row, obs_ens, obs_pos[:, None, :], innov_weight, jnp.swapaxes(block_rows, 1, 2))


def solution(mesh):
    in_specs = (
        P("half", ("rows", "obs"), None),
        P(("rows", "obs")),
        P(None, "half", ("rows", "obs"), None),
        P(None, ("rows", "obs")),
        P(None, "half", ("rows", "obs"), None),
        P(),
    )
    out_specs = P("half", ("rows", "obs"), None)
    return jax.shard_map(functools.partial(local, dict(mesh.shape)), mesh=mesh, in_specs=in_specs,
                         out_specs=out_specs, check_vma=False)
```
